32 devices in a mesh: chaos: 8 (over z, y), mesh: 4 (over x, core).
Axes of the slice: x: 2, y: 2, z: 4, core: 2. Of those that a mesh axis runs over, the one named last changes fastest.
Arguments:
- coefficients: bfloat16 [128, 96, 320], P('mesh', None, 'chaos'), may hold values from -6 to 6
- stiffness: bfloat16 [11, 12288, 6, 96], P(None, ('mesh', 'chaos')), may hold values from -0.25 to 0.25
- columns: int32 [128, 6], P('mesh'), may hold values from 0 to 127
- pair_rows: int32 [11, 1280], replicated, may hold values from 0 to 319
- pair_cols: int32 [11, 1280], replicated, may hold values from 0 to 319
- pair_vals: float32 [11, 1280], replicated, may hold values from -2 to 2
Outputs:
- applied: bfloat16 [128, 96, 320], P('mesh', None, 'chaos')
The draws below stay inside these ranges and needn't reach their ends.
All inputs are finite; a program needn't handle non-finite values.
Results may differ from the reference program's by a relative error of at most 0.001.
Values may be sent and summed in bfloat16 or wider, within the bound.
A program may use at most 320 MiB of HBM per device.

```python
import jax
import jax.numpy as jnp
from jax import lax

BLOCK = 96
MODES = 11
P_SIZE = 320
NNZ = 6
NODES = 128
PAIRS = 1280


def place_ends(entries, stream_key, least, largest):
    extent = entries.shape
    index_at = [jax.random.randint(jax.random.fold_in(stream_key, axis), (), 0, extent[axis]) for axis in range(len(extent))]
    entries = entries.at[tuple(index_at)].set(least)
    longest = extent.index(max(extent))
    index_at[longest] = (index_at[longest] + 1) % extent[longest]
    return entries.at[tuple(index_at)].set(largest)


def block_scale(stream_key, extent, pieces, low, top_value):
    level, own = 1.0, jax.random.fold_in(stream_key, 6)
    for axis_at, blocks in pieces:
        heights = jnp.exp(jax.random.uniform(jax.random.fold_in(own, axis_at), (blocks,), jnp.float32, low / len(pieces), top_value / len(pieces)))
        level = level * jnp.repeat(heights, extent[axis_at] // blocks).reshape([-1 if axis == axis_at else 1 for axis in range(len(extent))])
    return level


def normal_values(stream_key, shape, spread, bound, shards=(), kind=jnp.bfloat16):
    factor_of = block_scale(stream_key, shape, shards, -0.22, 0.18) if shards else 1.0
    array = jax.random.normal(stream_key, shape, jnp.float32) * spread * factor_of
    return jnp.minimum(jnp.maximum(array, -bound), bound).astype(kind)


def setup_inputs(seed: int = 0) -> dict:
    key_of = jax.random.split(jax.random.key(seed), 7)
    return {
        "coefficients": normal_values(key_of[0], (NODES, BLOCK, P_SIZE), 1.0, 6.0, ((0, 4), (2, 8))),
        "stiffness": normal_values(key_of[1], (MODES, NODES * BLOCK, NNZ, BLOCK), (NNZ * BLOCK) ** -0.5, 0.25, ((1, 32),)),
        "columns": place_ends(jax.random.randint(key_of[2], (NODES, NNZ), 0, NODES), jax.random.fold_in(key_of[2], 1), 0, NODES - 1).astype(jnp.int32),
        "pair_rows": place_ends(jax.random.randint(key_of[3], (MODES, PAIRS), 0, P_SIZE), jax.random.fold_in(key_of[3], 1), 0, P_SIZE - 1).astype(jnp.int32),
        "pair_cols": place_ends(jax.random.randint(key_of[4], (MODES, PAIRS), 0, P_SIZE), jax.random.fold_in(key_of[4], 1), 0, P_SIZE - 1).astype(jnp.int32),
        "pair_vals": normal_values(key_of[5], (MODES, PAIRS), 0.15, 2.0, (), jnp.float32),
    }


def reference(coefficients, stiffness, columns, pair_rows, pair_cols, pair_vals):
    mode_index = jnp.broadcast_to(jnp.arange(MODES, dtype=jnp.int32)[:, None], pair_rows.shape)
    coupling = jnp.zeros((MODES, P_SIZE, P_SIZE), jnp.float32).at[mode_index, pair_cols, pair_rows].add(pair_vals.astype(jnp.float32))
    picked = coefficients[columns].astype(jnp.float32)
    blocks = stiffness.reshape(MODES, NODES, BLOCK, NNZ, BLOCK)
    applied = jnp.zeros((NODES, BLOCK, P_SIZE), jnp.float32)
    for mode in range(MODES):
        products = jnp.einsum('rasb,rsbj->raj', blocks[mode].astype(jnp.float32), picked)
        applied = applied + jnp.einsum('raj,ji->rai', products, coupling[mode], precision=lax.Precision.HIGHEST)
    return applied.astype(jnp.bfloat16)
```

```python
import functools

import jax
import jax.numpy as jnp
from jax import lax
from jax.experimental import pallas as pl
from jax.experimental.pallas import tpu as pltpu
from jax.sharding import PartitionSpec as P

LANES = 128
VMEM_BYTES = 56 * 1024 * 1024


def split(value):
    high = value.astype(jnp.bfloat16)
    low = (value - high.astype(jnp.float32)).astype(jnp.bfloat16)
    return high, low


def coupling_kernel(rows_ref, cols_ref, vals_ref, high_ref, low_ref):
    total, pairs = high_ref.shape[1], rows_ref.shape[2]
    targets = lax.broadcasted_iota(jnp.int32, (total, pairs), 0)
    every_row = jnp.where(targets == rows_ref[0], 1.0, 0.0).astype(jnp.bfloat16)
    hit = targets == cols_ref[0]
    value_high, value_low = split(vals_ref[0])
    contract = (((1,), (1,)), ((), ()))
    result = jnp.zeros((total, total), jnp.float32)
    for part in (value_high, value_low):
        weighted = jnp.where(hit, part.astype(jnp.float32), 0.0).astype(jnp.bfloat16)
        result += lax.dot_general(
            every_row, weighted, contract, preferred_element_type=jnp.float32
        )
    high_ref[0], low_ref[0] = split(result)


def coupling_of(pair_rows, pair_cols, pair_vals, total):
    modes, pairs = pair_rows.shape
    entry = pl.BlockSpec((1, 1, pairs), lambda k: (k, 0, 0))
    matrix = pl.BlockSpec((1, total, total), lambda k: (k, 0, 0))
    high, low = pl.pallas_call(
        coupling_kernel,
        grid=(modes,),
        in_specs=[entry] * 3,
        out_specs=[matrix] * 2,
        out_shape=[jax.ShapeDtypeStruct((modes, total, total), jnp.bfloat16)] * 2,
        compiler_params=pltpu.CompilerParams(vmem_limit_bytes=VMEM_BYTES),
        cost_estimate=pl.CostEstimate(
            flops=4 * modes * pairs * total * total,
            bytes_accessed=4 * modes * total * total,
            transcendentals=0,
        ),
    )(pair_rows[:, None], pair_cols[:, None], pair_vals[:, None])
    both = jnp.stack([high, low])
    return both.transpose(0, 2, 1, 3).reshape(2 * total, modes * total)


def spread_kernel(stiff_ref, out_ref):
    _, nnz, block, _ = stiff_ref.shape
    nodes = out_ref.shape[0]
    width = stiff_ref.shape[3] // nodes
    out_ref[...] = jnp.zeros_like(out_ref)
    for s in range(nnz):
        slab = stiff_ref[0, s]
        for n in range(nodes):
            out_ref[n, s * LANES : s * LANES + block, :width] = slab[
                :, n * width : (n + 1) * width
            ]


def spread(stiff, nodes):
    modes, nnz, block, rows = stiff.shape
    return pl.pallas_call(
        spread_kernel,
        grid=(modes,),
        in_specs=[pl.BlockSpec((1, nnz, block, rows), lambda k: (k, 0, 0, 0))],
        out_specs=pl.BlockSpec((nodes, nnz * LANES, LANES), lambda k: (0, 0, k)),
        out_shape=jax.ShapeDtypeStruct(
            (nodes, nnz * LANES, modes * LANES), jnp.bfloat16
        ),
        compiler_params=pltpu.CompilerParams(vmem_limit_bytes=VMEM_BYTES),
        cost_estimate=pl.CostEstimate(
            flops=0, bytes_accessed=8 * modes * nnz * block * rows, transcendentals=0
        ),
    )(stiff)


def pick_kernel(wanted_ref, whole_ref, out_ref):
    @pl.loop(0, out_ref.shape[0])
    def _(at):
        out_ref[at] = whole_ref[wanted_ref[at]]


def pick(wanted, whole):
    return pl.pallas_call(
        pick_kernel,
        in_specs=[
            pl.BlockSpec(memory_space=pltpu.SMEM),
            pl.BlockSpec(memory_space=pltpu.VMEM),
        ],
        out_specs=pl.BlockSpec(memory_space=pltpu.VMEM),
        out_shape=jax.ShapeDtypeStruct(wanted.shape + whole.shape[1:], whole.dtype),
        compiler_params=pltpu.CompilerParams(vmem_limit_bytes=VMEM_BYTES),
    )(wanted, whole)


def apply_kernel(
    nnz, picked_ref, stiff_ref, coupling_ref, out_ref, gathered, high_ref, low_ref
):
    nodes, total, width = out_ref.shape
    block = picked_ref.shape[2]
    modes = stiff_ref.shape[2] // LANES
    group = high_ref.shape[1] // LANES
    gathered[...] = jnp.zeros_like(gathered)
    for first in range(0, nodes, group):
        for g in range(group):
            n = first + g
            for s in range(nnz):
                gathered[:, s * LANES : s * LANES + block] = picked_ref[n * nnz + s]
            lanes = slice(g * LANES, (g + 1) * LANES)
            for k in range(0, modes, 2):
                count = min(2, modes - k)
                product = jnp.dot(
                    gathered[...],
                    stiff_ref[n, :, k * LANES : (k + count) * LANES],
                    preferred_element_type=jnp.float32,
                )
                high, low = split(product)
                for c in range(count):
                    rows = slice((k + c) * total, (k + c + 1) * total)
                    high_ref[rows, lanes] = high[:, c * LANES : (c + 1) * LANES]
                    low_ref[rows, lanes] = low[:, c * LANES : (c + 1) * LANES]
        wide = jnp.dot(
            coupling_ref[...], high_ref[...], preferred_element_type=jnp.float32
        )
        narrow = jnp.dot(
            coupling_ref[:total], low_ref[...], preferred_element_type=jnp.float32
        )
        done = (wide[:total] + (wide[total:] + narrow)).astype(out_ref.dtype)
        for g in range(group):
            out_ref[first + g] = done[:, g * LANES : g * LANES + width]


def apply(picked, stiff, coupling, nnz, width):
    nodes = stiff.shape[0]
    total = picked.shape[1]
    modes = stiff.shape[2] // LANES
    group = 2 if nodes % 2 == 0 else 1
    return pl.pallas_call(
        functools.partial(apply_kernel, nnz),
        in_specs=[pl.BlockSpec(memory_space=pltpu.VMEM)] * 3,
        out_specs=pl.BlockSpec(memory_space=pltpu.VMEM),
        out_shape=jax.ShapeDtypeStruct((nodes, total, width), jnp.bfloat16),
        scratch_shapes=[
            pltpu.VMEM((total, nnz * LANES), jnp.bfloat16),
            pltpu.VMEM((modes * total, group * LANES), jnp.bfloat16),
            pltpu.VMEM((modes * total, group * LANES), jnp.bfloat16),
        ],
        compiler_params=pltpu.CompilerParams(vmem_limit_bytes=VMEM_BYTES),
        cost_estimate=pl.CostEstimate(
            flops=8 * nodes * LANES * modes * total * total,
            bytes_accessed=2 * (picked.size + stiff.size + coupling.size),
            transcendentals=0,
        ),
    )(picked, stiff, coupling)


def local(coefficients, stiffness, columns, pair_rows, pair_cols, pair_vals):
    node_count, block, own = coefficients.shape
    row_count = stiffness.shape[1]
    nnz = columns.shape[1]
    peers = lax.axis_size("chaos")
    total = own * peers
    assert row_count % block == 0 or block % row_count == 0
    span = max(1, row_count // block)
    width = row_count // span

    whole = lax.all_gather(coefficients.transpose(0, 2, 1), "mesh", axis=0, tiled=True)
    wanted = jnp.repeat(columns, block // width, axis=0).reshape(-1) if width < block else columns.reshape(-1)
    outgoing = pick(wanted, whole).reshape(peers, span * nnz, own, block)
    received = lax.all_to_all(outgoing, "chaos", split_axis=0, concat_axis=0, tiled=True)
    picked = received.transpose(1, 0, 2, 3).reshape(span * nnz, total, block)

    stiff = spread(stiffness.transpose(0, 2, 3, 1), span)
    coupling = coupling_of(pair_rows, pair_cols, pair_vals, total)
    finished = apply(picked, stiff, coupling, nnz, width)

    finished = finished.reshape(span, peers, own, width).transpose(1, 0, 2, 3)
    returned = lax.all_to_all(finished, "chaos", split_axis=0, concat_axis=0, tiled=True)
    if width < block:
        returned = returned.reshape(node_count, block // width, own, width)
        return returned.transpose(0, 1, 3, 2).reshape(node_count, block, own)
    return returned.reshape(node_count, own, block).transpose(0, 2, 1)


def solution(mesh):
    return jax.shard_map(
        local,
        mesh=mesh,
        in_specs=(
            P("mesh", None, "chaos"),
            P(None, ("mesh", "chaos"), None, None),
            P("mesh", None),
            P(),
            P(),
            P(),
        ),
        out_specs=P("mesh", None, "chaos"),
        check_vma=False,
    )
```

```python
import functools

import jax
import jax.numpy as jnp
from jax import lax
from jax.experimental import pallas as pl
from jax.experimental.pallas import tpu as pltpu
from jax.sharding import PartitionSpec as P

LANES = 128
VMEM_BYTES = 60 * 1024 * 1024
MESH = pl.DeviceIdType.MESH


def split(value):
    high = value.astype(jnp.bfloat16)
    low = (value - high.astype(jnp.float32)).astype(jnp.bfloat16)
    return high, low


def remote(source, target, send, receive, axis, peer):
    return pltpu.make_async_remote_copy(
        src_ref=source,
        dst_ref=target,
        send_sem=send,
        recv_sem=receive,
        device_id={axis: peer},
        device_id_type=MESH,
    )


def kernel(
    peers,
    parts,
    wanted_ref,
    own_ref,
    stiff_hbm,
    rows_ref,
    cols_ref,
    vals_ref,
    out_ref,
    whole,
    outgoing,
    received,
    finished,
    stiff,
    spread,
    coupling,
    wide_pick,
    picked,
    high_ref,
    low_ref,
    stiff_sem,
    part_send,
    part_recv,
    pick_send,
    pick_recv,
    done_send,
    done_recv,
):
    me, part = lax.axis_index("chaos"), lax.axis_index("mesh")
    nodes, own, block = own_ref.shape
    modes, nnz, _, row_count = stiff.shape
    span, width = out_ref.shape[1], out_ref.shape[3]
    total = peers * own
    padded = coupling.shape[1] // modes
    pairs = rows_ref.shape[1]
    group = high_ref.shape[1] // LANES

    barrier = pltpu.get_barrier_semaphore()

    @pl.loop(1, parts)
    def _(step):
        pl.semaphore_signal(barrier, inc=1, device_id={"mesh": lax.rem(part + step, parts)}, device_id_type=MESH)

    @pl.loop(1, peers)
    def _(step):
        pl.semaphore_signal(barrier, inc=1, device_id={"chaos": lax.rem(me + step, peers)}, device_id_type=MESH)

    stiff_copy = pltpu.make_async_copy(stiff_hbm, stiff, stiff_sem)
    stiff_copy.start()
    pl.semaphore_wait(barrier, parts + peers - 2)

    def part_copy(step):
        slot = pl.ds(part * nodes, nodes)
        return remote(own_ref, whole.at[slot], part_send.at[step], part_recv.at[step], "mesh", lax.rem(part + step, parts))

    @pl.loop(1, parts)
    def _(step):
        part_copy(step).start()

    whole[pl.ds(part * nodes, nodes)] = own_ref[...]

    spread[...] = jnp.zeros_like(spread)
    stiff_copy.wait()

    @pl.loop(0, modes)
    def _(k):
        for s in range(nnz):
            slab = stiff[k, s]
            for n in range(span):
                spread[k, n, s * LANES : s * LANES + block, :width] = slab[:, n * width : (n + 1) * width]

    @pl.loop(1, parts)
    def _(step):
        part_copy(step).wait()

    count = span * nnz

    def pick_copy(step):
        peer = lax.rem(me + step, peers)
        return remote(outgoing.at[peer], received.at[me], pick_send.at[step], pick_recv.at[step], "chaos", peer)

    @pl.loop(1, peers)
    def _(step):
        peer = lax.rem(me + step, peers)
        for at in range(count):
            outgoing[peer, at] = whole[wanted_ref[peer * count + at]]
        pick_copy(step).start()

    for at in range(count):
        received[me, at] = whole[wanted_ref[me * count + at]]

    @pl.loop(0, modes)
    def _(k):
        target_row = lax.broadcasted_iota(jnp.int32, (total, pairs), 0)
        target_col = lax.broadcasted_iota(jnp.int32, (padded, pairs), 0)
        at = pl.ds(k, 1)
        every_row = jnp.where(target_row == rows_ref[at], 1.0, 0.0).astype(jnp.bfloat16)
        hit = target_col == cols_ref[at]
        result = jnp.zeros((total, padded), jnp.float32)
        for value in split(vals_ref[at]):
            weighted = jnp.where(hit, value.astype(jnp.float32), 0.0).astype(jnp.bfloat16)
            result += lax.dot_general(
                every_row, weighted, (((1,), (1,)), ((), ())), preferred_element_type=jnp.float32
            )
        lanes = pl.ds(pl.multiple_of(k * padded, LANES), padded)
        coupling[:total, lanes], coupling[total:, lanes] = split(result)

    wide_pick[...] = jnp.zeros_like(wide_pick)
    if padded > total:
        for k in range(modes):
            gap = slice(k * padded + total, (k + 1) * padded)
            high_ref[gap] = jnp.zeros_like(high_ref[gap])
            low_ref[gap] = jnp.zeros_like(low_ref[gap])

    @pl.loop(1, peers)
    def _(step):
        pick_copy(step).wait()

    def done_copy(turn, step):
        peer = lax.rem(me + step, peers)
        slot = pl.ds(turn * group, group)
        return remote(
            finished.at[peer, slot], out_ref.at[me, slot], done_send.at[turn, step], done_recv.at[turn, step], "chaos", peer
        )

    for turn in range(span // group):
        for g in range(group):
            n = turn * group + g
            for s in range(nnz):
                for c in range(peers):
                    wide_pick[c * own : (c + 1) * own, s * LANES : s * LANES + block] = received[c, n * nnz + s].astype(jnp.float32)
            picked[...] = wide_pick[...].astype(jnp.bfloat16)
            lanes = slice(g * LANES, (g + 1) * LANES)
            for k in range(0, modes, 2):
                some = min(2, modes - k)
                weights = jnp.concatenate([spread[k + c, n] for c in range(some)], axis=1)
                high, low = split(jnp.dot(picked[...], weights, preferred_element_type=jnp.float32))
                for c in range(some):
                    rows = slice((k + c) * padded, (k + c) * padded + total)
                    high_ref[rows, lanes] = high[:, c * LANES : (c + 1) * LANES]
                    low_ref[rows, lanes] = low[:, c * LANES : (c + 1) * LANES]
        wide = jnp.dot(coupling[...], high_ref[...], preferred_element_type=jnp.float32)
        narrow = jnp.dot(coupling[:total], low_ref[...], preferred_element_type=jnp.float32)
        done = wide[:total] + (wide[total:] + narrow)
        for g in range(group):
            for c in range(peers):
                finished[c, turn * group + g] = done[c * own : (c + 1) * own, g * LANES : g * LANES + width].astype(jnp.bfloat16)

        @pl.loop(1, peers)
        def _(step):
            done_copy(turn, step).start()

        slot = pl.ds(turn * group, group)
        out_ref[me, slot] = finished[me, slot]

    for turn in range(span // group):

        @pl.loop(1, peers)
        def _(step):
            done_copy(turn, step).wait()


def local(coefficients, stiffness, columns, pair_rows, pair_cols, pair_vals):
    node_count, block, own = coefficients.shape
    modes, row_count, nnz, _ = stiffness.shape
    peers, parts = lax.axis_size("chaos"), lax.axis_size("mesh")
    total = own * peers
    assert row_count % block == 0 or block % row_count == 0
    span = max(1, row_count // block)
    width = row_count // span
    group = 2 if span % 2 == 0 else 1
    padded = -(-total // LANES) * LANES
    wanted = jnp.repeat(columns, block // width, axis=0).reshape(-1)
    bf16 = jnp.bfloat16
    vmem = pl.BlockSpec(memory_space=pltpu.VMEM)
    returned = pl.pallas_call(
        functools.partial(kernel, peers, parts),
        in_specs=[
            pl.BlockSpec(memory_space=pltpu.SMEM),
            vmem,
            pl.BlockSpec(memory_space=pl.ANY),
            vmem,
            vmem,
            vmem,
        ],
        out_specs=vmem,
        out_shape=jax.ShapeDtypeStruct((peers, span, own, width), bf16),
        scratch_shapes=[
            pltpu.VMEM((parts * node_count, own, block), bf16),
            pltpu.VMEM((peers, span * nnz, own, block), bf16),
            pltpu.VMEM((peers, span * nnz, own, block), bf16),
            pltpu.VMEM((peers, span, own, width), bf16),
            pltpu.VMEM((modes, nnz, block, row_count), bf16),
            pltpu.VMEM((modes, span, nnz * LANES, LANES), bf16),
            pltpu.VMEM((2 * total, modes * padded), bf16),
            pltpu.VMEM((total, nnz * LANES), jnp.float32),
            pltpu.VMEM((total, nnz * LANES), bf16),
            pltpu.VMEM((modes * padded, group * LANES), bf16),
            pltpu.VMEM((modes * padded, group * LANES), bf16),
            pltpu.SemaphoreType.DMA,
            pltpu.SemaphoreType.DMA((parts,)),
            pltpu.SemaphoreType.DMA((parts,)),
            pltpu.SemaphoreType.DMA((peers,)),
            pltpu.SemaphoreType.DMA((peers,)),
            pltpu.SemaphoreType.DMA((span // group, peers)),
            pltpu.SemaphoreType.DMA((span // group, peers)),
        ],
        compiler_params=pltpu.CompilerParams(
            collective_id=0, has_side_effects=True, vmem_limit_bytes=VMEM_BYTES
        ),
    )(
        wanted,
        coefficients.transpose(0, 2, 1),
        stiffness.transpose(0, 2, 3, 1),
        pair_rows,
        pair_cols,
        pair_vals,
    )
    if width < block:
        returned = returned.reshape(node_count, block // width, own, width)
        return returned.transpose(0, 1, 3, 2).reshape(node_count, block, own)
    return returned.reshape(node_count, own, block).transpose(0, 2, 1)


def solution(mesh):
    return jax.shard_map(
        local,
        mesh=mesh,
        in_specs=(
            P("mesh", None, "chaos"),
            P(None, ("mesh", "chaos"), None, None),
            P("mesh", None),
            P(),
            P(),
            P(),
        ),
        out_specs=P("mesh", None, "chaos"),
        check_vma=False,
    )
```

```python
import functools

import jax
import jax.numpy as jnp
from jax import lax
from jax.experimental import pallas as pl
from jax.experimental.pallas import tpu as pltpu
from jax.sharding import PartitionSpec as P

LANES = 128
VMEM_BYTES = 60 * 1024 * 1024
MESH = pl.DeviceIdType.MESH


def split(value):
    high = value.astype(jnp.bfloat16)
    low = (value - high.astype(jnp.float32)).astype(jnp.bfloat16)
    return high, low


def remote(source, target, send, receive, axis, peer):
    return pltpu.make_async_remote_copy(
        src_ref=source,
        dst_ref=target,
        send_sem=send,
        recv_sem=receive,
        device_id={axis: peer},
        device_id_type=MESH,
    )


def kernel(
    peers,
    parts,
    wanted_ref,
    own_ref,
    stiff_hbm,
    rows_ref,
    cols_ref,
    vals_ref,
    out_ref,
    gathered,
    whole,
    outgoing,
    received,
    finished,
    stiff,
    spread,
    coupling,
    wide_pick,
    picked,
    high_ref,
    low_ref,
    stiff_sem,
    part_send,
    part_recv,
    pick_send,
    pick_recv,
    done_send,
    done_recv,
):
    me, part = lax.axis_index("chaos"), lax.axis_index("mesh")
    nodes, own, block = own_ref.shape
    modes, nnz, _, row_count = stiff.shape
    span, width = out_ref.shape[1], out_ref.shape[3]
    total = peers * own
    padded = coupling.shape[1] // modes
    pairs = rows_ref.shape[1]
    group = high_ref.shape[1] // LANES

    barrier = pltpu.get_barrier_semaphore()

    @pl.loop(1, parts)
    def _(step):
        pl.semaphore_signal(barrier, inc=1, device_id={"mesh": lax.rem(part + step, parts)}, device_id_type=MESH)

    @pl.loop(1, peers)
    def _(step):
        pl.semaphore_signal(barrier, inc=1, device_id={"chaos": lax.rem(me + step, peers)}, device_id_type=MESH)

    stiff_copy = pltpu.make_async_copy(stiff_hbm, stiff, stiff_sem)
    stiff_copy.start()
    pl.semaphore_wait(barrier, parts + peers - 2)

    pack = gathered.shape[3] // block
    half = parts // 2
    partner = part + 1 - 2 * lax.rem(part, 2)

    def part_copy(slot, peer, at):
        return remote(gathered.at[slot], gathered.at[slot], part_send.at[at], part_recv.at[at], "mesh", peer)

    def same_copy(step):
        return part_copy(part, lax.rem(part + 2 * step, parts), step)

    def forward_copy(step):
        return part_copy(lax.rem(part + parts - 2 * step, parts), partner, half + step)

    for n in range(nodes):
        lanes = slice(n % pack * block, (n % pack + 1) * block)
        gathered[part, n // pack, :, lanes] = own_ref[n]

    for step in range(1, half):
        same_copy(step).start()
    part_copy(part, partner, 0).start()

    spread[...] = jnp.zeros_like(spread)
    stiff_copy.wait()

    @pl.loop(0, modes)
    def _(k):
        for s in range(nnz):
            slab = stiff[k, s]
            for n in range(span):
                spread[k, n, s * block : (s + 1) * block, :width] = slab[:, n * width : (n + 1) * width]

    for step in range(1, half):
        same_copy(step).wait()
        forward_copy(step).start()
    part_copy(part, partner, 0).wait()
    for step in range(1, half):
        forward_copy(step).wait()

    @pl.loop(0, parts)
    def _(p):
        for n in range(nodes):
            lanes = slice(n % pack * block, (n % pack + 1) * block)
            whole[p * nodes + n] = gathered[p, n // pack, :, lanes]

    share = block // width

    def pick(target, slot, peer):
        for n in range(span):
            node = peer * span // share + n
            for s in range(nnz):
                at = (n * nnz + s) * block
                target[slot, :, at : at + block] = whole[wanted_ref[s, node]]

    def pick_copy(step):
        peer = lax.rem(me + step, peers)
        return remote(outgoing.at[peer], received.at[me], pick_send.at[step], pick_recv.at[step], "chaos", peer)

    @pl.loop(1, peers)
    def _(turn):
        step = 1 + lax.rem(turn - 2 + peers // 2, peers - 1)
        peer = lax.rem(me + step, peers)
        pick(outgoing, peer, peer)
        pick_copy(step).start()

    pick(received, me, me)

    @pl.loop(0, modes)
    def _(k):
        target_row = lax.broadcasted_iota(jnp.int32, (total, pairs), 0)
        target_col = lax.broadcasted_iota(jnp.int32, (padded, pairs), 0)
        at = pl.ds(k, 1)
        every_row = jnp.where(target_row == rows_ref[at], 1.0, 0.0).astype(jnp.bfloat16)
        hit = target_col == cols_ref[at]
        result = jnp.zeros((total, padded), jnp.float32)
        for value in split(vals_ref[at]):
            weighted = jnp.where(hit, value.astype(jnp.float32), 0.0).astype(jnp.bfloat16)
            result += lax.dot_general(
                every_row, weighted, (((1,), (1,)), ((), ())), preferred_element_type=jnp.float32
            )
        lanes = pl.ds(pl.multiple_of(k * padded, LANES), padded)
        coupling[:total, lanes], coupling[total:, lanes] = split(result)

    if padded > total:
        for k in range(modes):
            gap = slice(k * padded + total, (k + 1) * padded)
            high_ref[gap] = jnp.zeros_like(high_ref[gap])
            low_ref[gap] = jnp.zeros_like(low_ref[gap])

    @pl.loop(1, peers)
    def _(step):
        pick_copy(step).wait()

    def done_copy(turn, step):
        peer = lax.rem(me + step, peers)
        slot = pl.ds(turn * group, group)
        return remote(
            finished.at[peer, slot], out_ref.at[me, slot], done_send.at[turn, step], done_recv.at[turn, step], "chaos", peer
        )

    for turn in range(span // group):
        for g in range(group):
            n = turn * group + g
            for c in range(peers):
                wide_pick[c * own : (c + 1) * own] = received[c, :, n * nnz * block : (n + 1) * nnz * block].astype(jnp.float32)
            picked[...] = wide_pick[...].astype(jnp.bfloat16)
            lanes = slice(g * LANES, (g + 1) * LANES)
            for k in range(0, modes, 2):
                some = min(2, modes - k)
                weights = jnp.concatenate([spread[k + c, n] for c in range(some)], axis=1)
                high, low = split(jnp.dot(picked[...], weights, preferred_element_type=jnp.float32))
                for c in range(some):
                    rows = slice((k + c) * padded, (k + c) * padded + total)
                    high_ref[rows, lanes] = high[:, c * LANES : (c + 1) * LANES]
                    low_ref[rows, lanes] = low[:, c * LANES : (c + 1) * LANES]
        wide = jnp.dot(coupling[...], high_ref[...], preferred_element_type=jnp.float32)
        narrow = jnp.dot(coupling[:total], low_ref[...], preferred_element_type=jnp.float32)
        done = wide[:total] + (wide[total:] + narrow)
        for g in range(group):
            for c in range(peers):
                finished[c, turn * group + g] = done[c * own : (c + 1) * own, g * LANES : g * LANES + width].astype(jnp.bfloat16)

        @pl.loop(1, peers)
        def _(step):
            done_copy(turn, step).start()

        slot = pl.ds(turn * group, group)
        out_ref[me, slot] = finished[me, slot]

    for turn in range(span // group):

        @pl.loop(1, peers)
        def _(step):
            done_copy(turn, step).wait()


def local(coefficients, stiffness, columns, pair_rows, pair_cols, pair_vals):
    node_count, block, own = coefficients.shape
    modes, row_count, nnz, _ = stiffness.shape
    peers, parts = lax.axis_size("chaos"), lax.axis_size("mesh")
    total = own * peers
    assert row_count % block == 0 or block % row_count == 0
    assert parts % 2 == 0
    span = max(1, row_count // block)
    width = row_count // span
    group = 2 if span % 2 == 0 else 1
    padded = -(-total // LANES) * LANES
    pack = 4 if node_count % 4 == 0 else 1
    bf16 = jnp.bfloat16
    vmem = pl.BlockSpec(memory_space=pltpu.VMEM)
    returned = pl.pallas_call(
        functools.partial(kernel, peers, parts),
        in_specs=[
            pl.BlockSpec(memory_space=pltpu.SMEM),
            vmem,
            pl.BlockSpec(memory_space=pl.ANY),
            vmem,
            vmem,
            vmem,
        ],
        out_specs=vmem,
        out_shape=jax.ShapeDtypeStruct((peers, span, own, width), bf16),
        scratch_shapes=[
            pltpu.VMEM((parts, node_count // pack, own, pack * block), bf16),
            pltpu.VMEM((parts * node_count, own, block), bf16),
            pltpu.VMEM((peers, own, span * nnz * block), bf16),
            pltpu.VMEM((peers, own, span * nnz * block), bf16),
            pltpu.VMEM((peers, span, own, width), bf16),
            pltpu.VMEM((modes, nnz, block, row_count), bf16),
            pltpu.VMEM((modes, span, nnz * block, LANES), bf16),
            pltpu.VMEM((2 * total, modes * padded), bf16),
            pltpu.VMEM((total, nnz * block), jnp.float32),
            pltpu.VMEM((total, nnz * block), bf16),
            pltpu.VMEM((modes * padded, group * LANES), bf16),
            pltpu.VMEM((modes * padded, group * LANES), bf16),
            pltpu.SemaphoreType.DMA,
            pltpu.SemaphoreType.DMA((parts,)),
            pltpu.SemaphoreType.DMA((parts,)),
            pltpu.SemaphoreType.DMA((peers,)),
            pltpu.SemaphoreType.DMA((peers,)),
            pltpu.SemaphoreType.DMA((span // group, peers)),
            pltpu.SemaphoreType.DMA((span // group, peers)),
        ],
        compiler_params=pltpu.CompilerParams(
            collective_id=0, has_side_effects=True, vmem_limit_bytes=VMEM_BYTES
        ),
    )(
        columns.T,
        coefficients.transpose(0, 2, 1),
        stiffness.transpose(0, 2, 3, 1),
        pair_rows,
        pair_cols,
        pair_vals,
    )
    if width < block:
        returned = returned.reshape(node_count, block // width, own, width)
        return returned.transpose(0, 1, 3, 2).reshape(node_count, block, own)
    return returned.reshape(node_count, own, block).transpose(0, 2, 1)


def solution(mesh):
    return jax.shard_map(
        local,
        mesh=mesh,
        in_specs=(
            P("mesh", None, "chaos"),
            P(None, ("mesh", "chaos"), None, None),
            P("mesh", None),
            P(),
            P(),
            P(),
        ),
        out_specs=P("mesh", None, "chaos"),
        check_vma=False,
    )
```

```python
import functools

import jax
import jax.numpy as jnp
from jax import lax
from jax.experimental import pallas as pl
from jax.experimental.pallas import tpu as pltpu
from jax.sharding import PartitionSpec as P

LANES = 128
VMEM_BYTES = 60 * 1024 * 1024
MESH = pl.DeviceIdType.MESH


def split(value):
    high = value.astype(jnp.bfloat16)
    low = (value - high.astype(jnp.float32)).astype(jnp.bfloat16)
    return high, low


def remote(source, target, send, receive, axis, peer):
    return pltpu.make_async_remote_copy(
        src_ref=source,
        dst_ref=target,
        send_sem=send,
        recv_sem=receive,
        device_id={axis: peer},
        device_id_type=MESH,
    )


def kernel(
    peers,
    parts,
    wanted_ref,
    own_ref,
    stiff_hbm,
    rows_ref,
    cols_ref,
    vals_ref,
    out_ref,
    gathered,
    whole,
    outgoing,
    received,
    finished,
    stiff,
    spread,
    coupling,
    wide_pick,
    picked,
    high_ref,
    low_ref,
    stiff_sem,
    part_send,
    part_recv,
    pick_send,
    pick_recv,
    done_send,
    done_recv,
):
    me, part = lax.axis_index("chaos"), lax.axis_index("mesh")
    nodes, own, block = own_ref.shape
    modes, nnz, _, row_count = stiff.shape
    span, width = out_ref.shape[1], out_ref.shape[3]
    total = peers * own
    padded = coupling.shape[1] // modes
    pairs = rows_ref.shape[1]
    group = high_ref.shape[1] // LANES

    barrier = pltpu.get_barrier_semaphore()

    @pl.loop(1, parts)
    def _(step):
        pl.semaphore_signal(barrier, inc=1, device_id={"mesh": lax.rem(part + step, parts)}, device_id_type=MESH)

    @pl.loop(1, peers)
    def _(step):
        pl.semaphore_signal(barrier, inc=1, device_id={"chaos": lax.rem(me + step, peers)}, device_id_type=MESH)

    stiff_copy = pltpu.make_async_copy(stiff_hbm, stiff, stiff_sem)
    stiff_copy.start()
    pl.semaphore_wait(barrier, parts + peers - 2)

    pack = gathered.shape[3] // block
    half = parts // 2
    partner = part + 1 - 2 * lax.rem(part, 2)

    def part_copy(slot, peer, at):
        return remote(gathered.at[slot], gathered.at[slot], part_send.at[at], part_recv.at[at], "mesh", peer)

    def same_copy(step):
        return part_copy(part, lax.rem(part + 2 * step, parts), step)

    def forward_copy(step):
        return part_copy(lax.rem(part + parts - 2 * step, parts), partner, half + step)

    for n in range(nodes):
        lanes = slice(n % pack * block, (n % pack + 1) * block)
        gathered[part, n // pack, :, lanes] = own_ref[n]

    for step in range(1, half):
        same_copy(step).start()
    part_copy(part, partner, 0).start()

    for step in range(1, half):
        same_copy(step).wait()
        forward_copy(step).start()
    part_copy(part, partner, 0).wait()
    for step in range(1, half):
        forward_copy(step).wait()

    @pl.loop(0, parts)
    def _(p):
        for n in range(nodes):
            lanes = slice(n % pack * block, (n % pack + 1) * block)
            whole[p * nodes + n] = gathered[p, n // pack, :, lanes]

    share = block // width

    def pick(target, slot, peer):
        for n in range(span):
            node = peer * span // share + n
            for s in range(nnz):
                at = (n * nnz + s) * block
                target[slot, :, at : at + block] = whole[wanted_ref[s, node]]

    def pick_copy(step):
        peer = lax.rem(me + step, peers)
        return remote(outgoing.at[peer], received.at[me], pick_send.at[step], pick_recv.at[step], "chaos", peer)

    @pl.loop(1, peers)
    def _(turn):
        step = 1 + lax.rem(turn - 2 + peers // 2, peers - 1)
        peer = lax.rem(me + step, peers)
        pick(outgoing, peer, peer)
        pick_copy(step).start()

    pick(received, me, me)

    spread[...] = jnp.zeros_like(spread)
    stiff_copy.wait()

    @pl.loop(0, modes)
    def _(k):
        for s in range(nnz):
            slab = stiff[k, s]
            for n in range(span):
                spread[k, n, s * block : (s + 1) * block, :width] = slab[:, n * width : (n + 1) * width]

    @pl.loop(0, modes)
    def _(k):
        target_row = lax.broadcasted_iota(jnp.int32, (total, pairs), 0)
        target_col = lax.broadcasted_iota(jnp.int32, (padded, pairs), 0)
        at = pl.ds(k, 1)
        every_row = jnp.where(target_row == rows_ref[at], 1.0, 0.0).astype(jnp.bfloat16)
        hit = target_col == cols_ref[at]
        result = jnp.zeros((total, padded), jnp.float32)
        for value in split(vals_ref[at]):
            weighted = jnp.where(hit, value.astype(jnp.float32), 0.0).astype(jnp.bfloat16)
            result += lax.dot_general(
                every_row, weighted, (((1,), (1,)), ((), ())), preferred_element_type=jnp.float32
            )
        lanes = pl.ds(pl.multiple_of(k * padded, LANES), padded)
        coupling[:total, lanes], coupling[total:, lanes] = split(result)

    if padded > total:
        for k in range(modes):
            gap = slice(k * padded + total, (k + 1) * padded)
            high_ref[gap] = jnp.zeros_like(high_ref[gap])
            low_ref[gap] = jnp.zeros_like(low_ref[gap])

    @pl.loop(1, peers)
    def _(step):
        pick_copy(step).wait()

    def done_copy(turn, step):
        peer = lax.rem(me + step, peers)
        slot = pl.ds(turn * group, group)
        return remote(
            finished.at[peer, slot], out_ref.at[me, slot], done_send.at[turn, step], done_recv.at[turn, step], "chaos", peer
        )

    for turn in range(span // group):
        for g in range(group):
            n = turn * group + g
            for c in range(peers):
                wide_pick[c * own : (c + 1) * own] = received[c, :, n * nnz * block : (n + 1) * nnz * block].astype(jnp.float32)
            picked[...] = wide_pick[...].astype(jnp.bfloat16)
            lanes = slice(g * LANES, (g + 1) * LANES)
            for k in range(0, modes, 2):
                some = min(2, modes - k)
                weights = jnp.concatenate([spread[k + c, n] for c in range(some)], axis=1)
                high, low = split(jnp.dot(picked[...], weights, preferred_element_type=jnp.float32))
                for c in range(some):
                    rows = slice((k + c) * padded, (k + c) * padded + total)
                    high_ref[rows, lanes] = high[:, c * LANES : (c + 1) * LANES]
                    low_ref[rows, lanes] = low[:, c * LANES : (c + 1) * LANES]
        wide = jnp.dot(coupling[...], high_ref[...], preferred_element_type=jnp.float32)
        narrow = jnp.dot(coupling[:total], low_ref[...], preferred_element_type=jnp.float32)
        done = wide[:total] + (wide[total:] + narrow)
        for g in range(group):
            for c in range(peers):
                finished[c, turn * group + g] = done[c * own : (c + 1) * own, g * LANES : g * LANES + width].astype(jnp.bfloat16)

        @pl.loop(1, peers)
        def _(step):
            done_copy(turn, step).start()

        slot = pl.ds(turn * group, group)
        out_ref[me, slot] = finished[me, slot]

    for turn in range(span // group):

        @pl.loop(1, peers)
        def _(step):
            done_copy(turn, step).wait()


def local(coefficients, stiffness, columns, pair_rows, pair_cols, pair_vals):
    node_count, block, own = coefficients.shape
    modes, row_count, nnz, _ = stiffness.shape
    peers, parts = lax.axis_size("chaos"), lax.axis_size("mesh")
    total = own * peers
    assert row_count % block == 0 or block % row_count == 0
    assert parts % 2 == 0
    span = max(1, row_count // block)
    width = row_count // span
    group = 2 if span % 2 == 0 else 1
    padded = -(-total // LANES) * LANES
    pack = 4 if node_count % 4 == 0 else 1
    bf16 = jnp.bfloat16
    vmem = pl.BlockSpec(memory_space=pltpu.VMEM)
    returned = pl.pallas_call(
        functools.partial(kernel, peers, parts),
        in_specs=[
            pl.BlockSpec(memory_space=pltpu.SMEM),
            vmem,
            pl.BlockSpec(memory_space=pl.ANY),
            vmem,
            vmem,
            vmem,
        ],
        out_specs=vmem,
        out_shape=jax.ShapeDtypeStruct((peers, span, own, width), bf16),
        scratch_shapes=[
            pltpu.VMEM((parts, node_count // pack, own, pack * block), bf16),
            pltpu.VMEM((parts * node_count, own, block), bf16),
            pltpu.VMEM((peers, own, span * nnz * block), bf16),
            pltpu.VMEM((peers, own, span * nnz * block), bf16),
            pltpu.VMEM((peers, span, own, width), bf16),
            pltpu.VMEM((modes, nnz, block, row_count), bf16),
            pltpu.VMEM((modes, span, nnz * block, LANES), bf16),
            pltpu.VMEM((2 * total, modes * padded), bf16),
            pltpu.VMEM((total, nnz * block), jnp.float32),
            pltpu.VMEM((total, nnz * block), bf16),
            pltpu.VMEM((modes * padded, group * LANES), bf16),
            pltpu.VMEM((modes * padded, group * LANES), bf16),
            pltpu.SemaphoreType.DMA,
            pltpu.SemaphoreType.DMA((parts,)),
            pltpu.SemaphoreType.DMA((parts,)),
            pltpu.SemaphoreType.DMA((peers,)),
            pltpu.SemaphoreType.DMA((peers,)),
            pltpu.SemaphoreType.DMA((span // group, peers)),
            pltpu.SemaphoreType.DMA((span // group, peers)),
        ],
        compiler_params=pltpu.CompilerParams(
            collective_id=0, has_side_effects=True, vmem_limit_bytes=VMEM_BYTES
        ),
    )(
        columns.T,
        coefficients.transpose(0, 2, 1),
        stiffness.transpose(0, 2, 3, 1),
        pair_rows,
        pair_cols,
        pair_vals,
    )
    if width < block:
        returned = returned.reshape(node_count, block // width, own, width)
        return returned.transpose(0, 1, 3, 2).reshape(node_count, block, own)
    return returned.reshape(node_count, own, block).transpose(0, 2, 1)


def solution(mesh):
    return jax.shard_map(
        local,
        mesh=mesh,
        in_specs=(
            P("mesh", None, "chaos"),
            P(None, ("mesh", "chaos"), None, None),
            P("mesh", None),
            P(),
            P(),
            P(),
        ),
        out_specs=P("mesh", None, "chaos"),
        check_vma=False,
    )
```
